256 devices in a mesh: ctx: 32 (over x, y, core), tp: 8 (over z).
Axes of the slice: x: 4, y: 4, z: 8, core: 2. Of those that a mesh axis runs over, the one named last changes fastest.
Arguments:
- q_in: bfloat16 [4096, 8192], P('ctx', 'tp'), may hold values from -6 to 6
- k_in: bfloat16 [4096, 8192], P('ctx', 'tp'), may hold values from -6 to 6
- v_in: bfloat16 [4096, 8192], P('ctx', 'tp'), may hold values from -6 to 6
- short_filter: float32 [3, 3, 8192], P(None, None, 'tp'), may hold values from -3 to 3
- rate: float32 [8192, 16], P('tp'), may hold values from 2.4414063e-05 to 0.05
- residue: float32 [8192, 16], P('tp'), may hold values from -0.3125 to 0.3125
- resid: bfloat16 [4096, 8192], P('ctx', 'tp'), may hold values from -18 to 18, as said below
- gain: float32 [8192], P('tp'), may hold values from 0.5 to 1.5
Outputs:
- normed: bfloat16 [4096, 8192], P('ctx', 'tp')
The draws below stay inside these ranges and needn't reach their ends.
Inputs may be any that keep to these rules, and one draw needn't show every extreme that they name: `resid`: residual stream entries; channel scales differ across the width.
All inputs are finite; a program needn't handle non-finite values.
Results may differ from the reference program's by a relative error of at most 0.0042.
Values may be sent and summed in bfloat16 or wider, within the bound.
A program may use at most 64 MiB of HBM per device.

```python
import math
import jax
import jax.numpy as jnp
from jax import lax

D = 8192
MODES = 16
SHORT = 3
SEQ = 4096


def draw_resid(key, part):
    ramp = jnp.arange(D, dtype=jnp.float32) / D
    base = jnp.clip(jax.random.normal(key, (SEQ, D), jnp.float32), -6.0, 6.0)
    scale = 1.0 + 2.0 * ramp
    return (base * scale[None, :]).astype(jnp.bfloat16)


def shard_levels(own_key, shape, cuts, smallest, high):
    factor_of, own = 1.0, jax.random.fold_in(own_key, 6)
    for dim, shards_of in cuts:
        heights = jnp.exp(jax.random.uniform(jax.random.fold_in(own, dim), (shards_of,), jnp.float32, smallest / len(cuts), high / len(cuts)))
        factor_of = factor_of * jnp.repeat(heights, shape[dim] // shards_of).reshape([-1 if axis == dim else 1 for axis in range(len(shape))])
    return factor_of


def centred(key, extent, deviation, limit, shards=(), held_as=jnp.bfloat16):
    entries = deviation * jax.random.normal(key, extent, jnp.float32)
    if shards:
        entries = entries * shard_levels(key, extent, shards, -0.22, 0.18)
    return jnp.clip(entries, -limit, limit).astype(held_as)


def setup_inputs(seed: int = 0) -> dict:
    key_list = jax.random.split(jax.random.key(seed), 9)
    q_in = centred(key_list[0], (SEQ, D), 1.0, 6.0, ((0, 32), (1, 8)))
    k_in = centred(key_list[1], (SEQ, D), 1.0, 6.0, ((0, 32), (1, 8)))
    v_in = centred(key_list[2], (SEQ, D), 1.0, 6.0, ((0, 32), (1, 8)))
    short_filter = centred(key_list[3], (3, SHORT, D), 0.5, 3.0, ((2, 8),), jnp.float32)
    rate = jnp.clip(jnp.exp(math.log(0.05) - 7.624619 * jax.random.uniform(key_list[4], (D, MODES), jnp.float32) ** shard_levels(key_list[4], (D, MODES), ((0, 8),), -0.2, 0.2)), 2.441406286379788e-05, 0.05)
    residue = centred(key_list[5], (D, MODES), 0.02, 0.3125, ((0, 8),), jnp.float32)
    resid = draw_resid(jax.random.fold_in(key_list[8], 71), 0)
    gain = jnp.clip(1.0 + 0.1 * jax.random.normal(key_list[7], (D,), jnp.float32), 0.5, 1.5)
    return {"q_in": q_in, "k_in": k_in, "v_in": v_in, "short_filter": short_filter, "rate": rate, "residue": residue, "resid": resid, "gain": gain}


def short_conv(stream, taps):
    values = stream.astype(jnp.float32)
    out = taps[0] * values
    for j in range(1, SHORT):
        shifted = jnp.concatenate([jnp.zeros((j, values.shape[1]), jnp.float32), values[:-j]], axis=0)
        out = out + taps[j] * shifted
    return out

def long_conv(gated, rate, residue):
    length = gated.shape[0]
    group = min(256, D)
    times = jnp.arange(length, dtype=jnp.int32).astype(jnp.float32)

    def one_group(index):
        start = (index * group).astype(jnp.int32)
        columns = lax.dynamic_slice_in_dim(gated, start, group, 1).astype(jnp.float32).T
        rates = lax.dynamic_slice_in_dim(rate, start, group, 0)
        weights = lax.dynamic_slice_in_dim(residue, start, group, 0)
        filt = jnp.zeros((group, length), jnp.float32)
        for m in range(MODES):
            filt = filt + weights[:, m:m + 1] * jnp.exp(-rates[:, m:m + 1] * times[None, :])
        spectrum = jnp.fft.rfft(columns, n=2 * length, axis=1) * jnp.fft.rfft(filt, n=2 * length, axis=1)
        return jnp.fft.irfft(spectrum, n=2 * length, axis=1)[:, :length]
    pieces = lax.map(one_group, jnp.arange(D // group, dtype=jnp.int32))
    return pieces.reshape(D, length).T

def reference(q_in, k_in, v_in, short_filter, rate, residue, resid, gain):
    q_feat = short_conv(q_in, short_filter[0])
    k_feat = short_conv(k_in, short_filter[1])
    v_feat = short_conv(v_in, short_filter[2])
    gated = lax.optimization_barrier((k_feat * v_feat).astype(jnp.bfloat16))
    mixed = long_conv(gated, rate, residue)
    stream = resid.astype(jnp.float32) + q_feat * mixed
    scale = lax.rsqrt(lax.optimization_barrier(jnp.sum(stream * stream, axis=1, keepdims=True)) / D + 1e-05)
    return (stream * scale * gain[None, :]).astype(jnp.bfloat16)
```

```python
import functools

import jax
import jax.numpy as jnp
from jax import lax
from jax.experimental import pallas as pl
from jax.experimental.pallas import tpu as pltpu
from jax.sharding import PartitionSpec as P

MESH = pl.DeviceIdType.MESH
D = 8192
ROWS = 128
WIDTH = 1024
LANES = 128
BLOCKS = WIDTH // LANES
MODES = 16
HALF = MODES // 2
TILES = ROWS // 8
F32 = jnp.float32
BF16 = jnp.bfloat16


def lanes_of(b):
    return pl.ds(pl.multiple_of(b * LANES, LANES), LANES)


def short_taps(sf_ref, stream, lanes):
    return [sf_ref[stream, pl.ds(j, 1), lanes] for j in range(3)]


def conv_block(values, taps):
    return taps[0] * values + taps[1] * pltpu.roll(values, 1, 0) + taps[2] * pltpu.roll(values, 2, 0)


def conv_top(values, taps, two_back, one_back):
    row = lax.broadcasted_iota(jnp.int32, values.shape, 0)
    once = jnp.where(row == 0, one_back, pltpu.roll(values, 1, 0))
    twice = jnp.where(row == 0, two_back, jnp.where(row == 1, one_back, pltpu.roll(values, 2, 0)))
    return taps[0] * values + taps[1] * once + taps[2] * twice


def mixer_kernel(
    q_hbm, k_hbm, v_hbm, sf_hbm, rate_hbm, res_hbm, resid_hbm, gain_hbm, out_ref,
    q_s, k_s, v_s, sf_s, rate_s, res_s, resid_s, gain_s,
    edge, halo, step_t, end_t, start_t, u_s, f_s, y_s, qf_s, st_s,
    e_own, e_mate, chip, yb1, xb1, yb2, xb2, zsend, zbuf, sq,
    load_sem, edge_sem, core_sem, y1s, y1r, x1s, x1r, y2s, y2r, x2s, x2r, zs, zr,
):
    ctx = lax.axis_index("ctx")
    tp = lax.axis_index("tp")
    x, y, core = ctx // 8, (ctx // 2) % 4, ctx % 2
    mate = ctx + 1 - 2 * core

    def y_peer(k):
        return x * 8 + ((y + k) % 4) * 2 + core

    def x_peer(k):
        return ((x + k) % 4) * 8 + y * 2 + core

    after, before = (ctx + 1) % 32, (ctx + 31) % 32

    barrier = pltpu.get_barrier_semaphore()
    greeted = [(mate, tp), (after, tp), (before, tp)]
    greeted += [(y_peer(k), tp) for k in (1, 2, 3)] + [(x_peer(k), tp) for k in (1, 2, 3)]
    greeted += [(ctx, (tp + k) % 8) for k in range(1, 8)]
    for who in greeted:
        pl.semaphore_signal(barrier, inc=1, device_id=who, device_id_type=MESH)

    loads = {}
    for i, (name, src, dst) in enumerate([
        ("rate", rate_hbm, rate_s), ("k", k_hbm, k_s), ("v", v_hbm, v_s), ("sf", sf_hbm, sf_s),
        ("q", q_hbm, q_s), ("res", res_hbm, res_s), ("resid", resid_hbm, resid_s), ("gain", gain_hbm, gain_s),
    ]):
        loads[name] = pltpu.make_async_copy(src, dst, load_sem.at[i])
        loads[name].start()

    def remote(src, dst, ssem, rsem, who):
        return pltpu.make_async_remote_copy(
            src_ref=src, dst_ref=dst, send_sem=ssem, recv_sem=rsem, device_id=who, device_id_type=MESH
        )

    loads["rate"].wait()

    @pl.loop(0, BLOCKS)
    def _(b):
        lanes = lanes_of(b)
        row = lax.broadcasted_iota(jnp.int32, (8, LANES), 0).astype(F32)
        for m in range(MODES):
            r = jnp.broadcast_to(rate_s[pl.ds(m, 1), lanes], (8, LANES))
            step_t[m, :, lanes] = jnp.exp(-8.0 * r)
            end_t[m, :, lanes] = jnp.exp((row - 7.0) * r)

    loads["k"].wait()
    loads["v"].wait()
    loads["sf"].wait()
    loads["q"].wait()
    edge[0:2, :] = k_s[ROWS - 16 : ROWS, :].astype(F32)[14:16]
    edge[2:4, :] = v_s[ROWS - 16 : ROWS, :].astype(F32)[14:16]
    edge[4:6, :] = q_s[ROWS - 16 : ROWS, :].astype(F32)[14:16]
    edge[6:8, :] = jnp.zeros((2, WIDTH), F32)

    pl.semaphore_wait(barrier, len(greeted))
    edge_copy = remote(edge, halo, edge_sem.at[0], edge_sem.at[1], (after, tp))
    edge_copy.start()

    @pl.loop(0, BLOCKS)
    def _(b):
        lanes = lanes_of(b)
        kf = conv_block(k_s[:, lanes].astype(F32), short_taps(sf_s, 1, lanes))
        vf = conv_block(v_s[:, lanes].astype(F32), short_taps(sf_s, 2, lanes))
        u = (kf * vf).astype(BF16).astype(F32)
        u_s[b] = u
        row = lax.broadcasted_iota(jnp.int32, (8, LANES), 0)
        step = step_t[:, :, lanes]
        first = jnp.where(row < 2, 0.0, u[0:8])
        g = jnp.broadcast_to(first[None], (MODES, 8, LANES))
        for i in range(1, TILES):
            g = step * g + u[8 * i : 8 * i + 8][None]
        e_own[:, lanes] = jnp.sum(end_t[:, :, lanes] * g, axis=1)

    edge_copy.wait()
    has_before = ctx > 0

    @pl.loop(0, BLOCKS)
    def _(b):
        lanes = lanes_of(b)
        past = jnp.where(has_before, halo[:, lanes], 0.0)
        kf = conv_top(k_s[0:16, lanes].astype(F32)[0:8], short_taps(sf_s, 1, lanes), past[0:1], past[1:2])
        vf = conv_top(v_s[0:16, lanes].astype(F32)[0:8], short_taps(sf_s, 2, lanes), past[2:3], past[3:4])
        u = (kf * vf).astype(BF16).astype(F32)
        u_s[b, 0:8, :] = u
        r = rate_s[:, lanes]
        e_own[:, lanes] = e_own[:, lanes] + jnp.exp(-127.0 * r) * u[0:1] + jnp.exp(-126.0 * r) * u[1:2]

    core_copy = remote(e_own, e_mate, core_sem.at[0], core_sem.at[1], (mate, tp))
    core_copy.start()

    loads["res"].wait()

    @pl.loop(0, BLOCKS)
    def _(b):
        lanes = lanes_of(b)
        row = lax.broadcasted_iota(jnp.int32, (8, LANES), 0).astype(F32)
        terms = []
        for m in range(MODES):
            r = jnp.broadcast_to(rate_s[pl.ds(m, 1), lanes], (8, LANES))
            w = jnp.broadcast_to(res_s[pl.ds(m, 1), lanes], (8, LANES))
            terms.append(w * jnp.exp(-row * r))
            start_t[m, :, lanes] = w * jnp.exp(-(row + 1.0) * r)
        v = jnp.stack(terms)
        step = step_t[:, :, lanes]
        for i in range(TILES):
            f_s[b, 8 * i : 8 * i + 8, :] = jnp.sum(v, axis=0)
            if i < TILES - 1:
                v = v * step

    core_copy.wait()
    rates = rate_s[...]
    one = jnp.exp(-128.0 * rates)
    mine, theirs = e_own[...], e_mate[...]
    first_core = jnp.where(core == 0, mine, theirs)
    second_core = jnp.where(core == 0, theirs, mine)
    chip[...] = one * first_core + second_core
    yb1[y] = chip[0:HALF, :]
    xb1[x] = chip[HALF:MODES, :]
    stage1 = []
    for k in (1, 2, 3):
        stage1.append(remote(chip.at[pl.ds(0, HALF)], yb1.at[y], y1s.at[k], y1r.at[y], (y_peer(k), tp)))
        stage1.append(remote(chip.at[pl.ds(HALF, HALF)], xb1.at[x], x1s.at[k], x1r.at[x], (x_peer(k), tp)))
    for c in stage1:
        c.start()

    def local_conv(b):
        u = u_s[b]
        row = lax.broadcasted_iota(jnp.int32, (8, LANES), 0)
        acc = [None] * TILES
        for shift in range(8):
            if shift == 0:
                moved = u
            else:
                moved = pltpu.roll(u, shift, 0)
                moved = jnp.concatenate([jnp.where(row < shift, 0.0, moved[0:8]), moved[8:]], axis=0)
            for p in range(TILES):
                tap = jnp.broadcast_to(f_s[b, pl.ds(8 * p + shift, 1), :], (8, LANES))
                for i in range(p, TILES):
                    term = tap * moved[8 * (i - p) : 8 * (i - p) + 8]
                    acc[i] = term if acc[i] is None else acc[i] + term
        for i in range(TILES):
            y_s[b, 8 * i : 8 * i + 8, :] = acc[i]

    @pl.loop(0, BLOCKS)
    def _(b):
        lanes = lanes_of(b)
        taps = short_taps(sf_s, 0, lanes)
        values = q_s[:, lanes].astype(F32)
        qf_s[b] = conv_block(values, taps)
        past = jnp.where(has_before, halo[:, lanes], 0.0)
        qf_s[b, 0:8, :] = conv_top(values[0:8], taps, past[4:5], past[5:6])

    @pl.loop(0, BLOCKS // 2)
    def _(b):
        local_conv(b)

    for k in (1, 2, 3):
        remote(chip.at[pl.ds(0, HALF)], yb1.at[(y + k) % 4], y1s.at[k], y1r.at[(y + k) % 4], (y_peer(k), tp)).wait_recv()
        remote(chip.at[pl.ds(0, HALF)], xb1.at[(x + k) % 4], x1s.at[k], x1r.at[(x + k) % 4], (x_peer(k), tp)).wait_recv()

    low, high = rate_s[0:HALF, :], rate_s[HALF:MODES, :]
    by_chip, by_row = jnp.exp(-256.0 * low), jnp.exp(-1024.0 * high)
    total = jnp.zeros((HALF, WIDTH), F32)
    row_part = total
    for i in range(4):
        row_part = jnp.where(y == i, total, row_part)
        total = by_chip * total + yb1[i]
    xb2[x] = total
    run = jnp.zeros((HALF, WIDTH), F32)
    column = run
    for i in range(4):
        column = jnp.where(x == i, run, column)
        run = by_row * run + xb1[i]
    yb2[y] = column
    st_s[0] = total
    st_s[1] = column
    st_s[2] = by_row * column + chip[HALF:MODES, :]
    stage2 = []
    for k in (1, 2, 3):
        stage2.append(remote(st_s.at[0], xb2.at[x], x2s.at[k], x2r.at[x], (x_peer(k), tp)))
        which = 1 + (3 - (y + k) // 4 * 3) // 3
        stage2.append(remote(st_s.at[which], yb2.at[y], y2s.at[k], y2r.at[y], (y_peer(k), tp)))
    for c in stage2:
        c.start()

    @pl.loop(BLOCKS // 2, BLOCKS)
    def _(b):
        local_conv(b)

    for k in (1, 2, 3):
        remote(st_s.at[0], xb2.at[(x + k) % 4], x2s.at[k], x2r.at[(x + k) % 4], (x_peer(k), tp)).wait_recv()
        remote(st_s.at[0], yb2.at[(y + k) % 4], y2s.at[k], y2r.at[(y + k) % 4], (y_peer(k), tp)).wait_recv()

    by_row_low = jnp.exp(-1024.0 * low)
    run = jnp.zeros((HALF, WIDTH), F32)
    rows_before = run
    for i in range(4):
        rows_before = jnp.where(x == i, run, rows_before)
        if i < 3:
            run = by_row_low * run + xb2[i]
    state_low = row_part + jnp.exp((-256.0 * y.astype(F32)) * low) * rows_before
    state_high = jnp.zeros((HALF, WIDTH), F32)
    for i in range(4):
        gap = ((y + 3 - i) % 4).astype(F32)
        state_high = state_high + jnp.exp((-256.0 * gap) * high) * yb2[i]
    state = jnp.concatenate([state_low, state_high], axis=0)
    state = jnp.where(core == 0, state, jnp.exp(-128.0 * rate_s[...]) * state + e_mate[...])
    e_own[...] = state

    loads["resid"].wait()
    sq[...] = jnp.zeros((ROWS, LANES), F32)

    @pl.loop(0, BLOCKS)
    def _(b):
        lanes = lanes_of(b)
        step = step_t[:, :, lanes]
        v = jnp.stack([
            start_t[m, :, lanes] * jnp.broadcast_to(e_own[pl.ds(m, 1), lanes], (8, LANES)) for m in range(MODES)
        ])
        for i in range(TILES):
            tile = pl.ds(8 * i, 8)
            mixed = y_s[b, tile, :] + jnp.sum(v, axis=0)
            if i < TILES - 1:
                v = v * step
            qf_s[b, tile, :] = qf_s[b, tile, :] * mixed
        stream = resid_s[:, lanes].astype(F32) + qf_s[b]
        y_s[b] = stream
        sq[...] = sq[...] + stream * stream

    ones = jnp.ones((8, LANES), F32)
    contract_lanes = (((1,), (1,)), ((), ()))
    sums = lax.dot_general(ones, sq[...], contract_lanes, precision=lax.Precision.HIGHEST, preferred_element_type=F32)
    zsend[...] = sums[0:1]
    zbuf[tp] = sums[0:1]
    zcopies = [
        remote(zsend, zbuf.at[tp], zs.at[k], zr.at[tp], (ctx, (tp + k) % 8)) for k in range(1, 8)
    ]
    for c in zcopies:
        c.start()
    loads["gain"].wait()
    for k in range(1, 8):
        remote(zsend, zbuf.at[(tp + k) % 8], zs.at[k], zr.at[(tp + k) % 8], (ctx, (tp + k) % 8)).wait_recv()
    parts = jnp.concatenate([zbuf[i] for i in range(8)], axis=0)
    squares = lax.dot_general(
        parts, ones, (((0,), (0,)), ((), ())), precision=lax.Precision.HIGHEST, preferred_element_type=F32
    )
    scale = lax.rsqrt(squares * (1.0 / D) + 1e-05)
    sq[...] = scale

    @pl.loop(0, BLOCKS)
    def _(b):
        lanes = lanes_of(b)
        out_ref[:, lanes] = (y_s[b] * sq[...] * gain_s[:, lanes]).astype(BF16)

    for c in stage1 + stage2 + zcopies:
        c.wait_send()


def per_device(q_in, k_in, v_in, short_filter, rate, residue, resid, gain):
    vm = pltpu.VMEM
    dma = pltpu.SemaphoreType.DMA
    any_spec = pl.BlockSpec(memory_space=pltpu.HBM)
    stream = (ROWS, WIDTH)
    table = (MODES, 8, WIDTH)
    blocks = (BLOCKS, ROWS, LANES)
    half4 = (4, HALF, WIDTH)
    return pl.pallas_call(
        mixer_kernel,
        out_shape=jax.ShapeDtypeStruct(stream, BF16),
        in_specs=[any_spec] * 8,
        out_specs=pl.BlockSpec(memory_space=pltpu.VMEM),
        scratch_shapes=[
            vm(stream, BF16), vm(stream, BF16), vm(stream, BF16), vm((3, 3, WIDTH), F32),
            vm((MODES, WIDTH), F32), vm((MODES, WIDTH), F32), vm(stream, BF16), vm((1, WIDTH), F32),
            vm((8, WIDTH), F32), vm((8, WIDTH), F32), vm(table, F32), vm(table, F32), vm(table, F32),
            vm(blocks, F32), vm(blocks, F32), vm(blocks, F32), vm(blocks, F32), vm((3, HALF, WIDTH), F32),
            vm((MODES, WIDTH), F32), vm((MODES, WIDTH), F32), vm((MODES, WIDTH), F32),
            vm(half4, F32), vm(half4, F32), vm(half4, F32), vm(half4, F32),
            vm((1, LANES), F32), vm((8, 1, LANES), F32), vm((ROWS, LANES), F32),
            dma((8,)), dma((2,)), dma((2,)),
            dma((4,)), dma((4,)), dma((4,)), dma((4,)), dma((4,)), dma((4,)), dma((4,)), dma((4,)),
            dma((8,)), dma((8,)),
        ],
        compiler_params=pltpu.CompilerParams(
            collective_id=0, has_side_effects=True, vmem_limit_bytes=48 * 1024 * 1024
        ),
        name="mixer",
    )(q_in, k_in, v_in, short_filter, rate.T, residue.T, resid, gain.reshape(1, WIDTH))


def solution(mesh):
    in_specs = (
        P("ctx", "tp"),
        P("ctx", "tp"),
        P("ctx", "tp"),
        P(None, None, "tp"),
        P("tp", None),
        P("tp", None),
        P("ctx", "tp"),
        P("tp"),
    )
    return jax.shard_map(
        per_device, mesh=mesh, in_specs=in_specs, out_specs=P("ctx", "tp"), check_vma=False
    )
```
